32 devices in a mesh: groups: 1, seq: 32 (over z, y, x, core), tp: 1.
Axes of the slice: x: 2, y: 2, z: 4, core: 2. Of those that a mesh axis runs over, the one named last changes fastest.
Arguments:
- resid: bfloat16 [6144, 3584], P(('groups', 'seq')), may hold values from -14 to 14
- gate_pre: bfloat16 [6144, 9472], P(('groups', 'seq'), 'tp'), may hold values from -6 to 6
- up_pre: bfloat16 [6144, 9472], P(('groups', 'seq'), 'tp'), may hold values from -6 to 6
- down_weight: bfloat16 [9472, 3584], P(('tp', 'seq')), may hold values from -0.0625 to 0.0625
- norm_gain: float32 [3584], replicated, may hold values from 0.1 to 1.9
- value_head: float32 [3584], replicated, may hold values from -0.09375 to 0.09375
- rewards: float32 [6144], P(('groups', 'seq')), may hold values from -0.12 to 0.12
- seg_ids: int32 [6144], P(('groups', 'seq')), may hold values from 0 to 7, never falling along the last dimension, each value on 1 to 1536 neighbouring positions
Outputs:
- values: float32 [6144], P(('groups', 'seq'))
- advantages: float32 [6144], P(('groups', 'seq'))
- grad_gate: bfloat16 [6144, 9472], P(('groups', 'seq'), 'tp')
- grad_up: bfloat16 [6144, 9472], P(('groups', 'seq'), 'tp')
- grad_resid: bfloat16 [6144, 3584], P(('groups', 'seq'))
The draws below stay inside these ranges and needn't reach their ends.
Inputs may be any that keep to these rules, and one draw needn't show every extreme that they name: `seg_ids`: never falls along the stream; each document holds 1 to 1536 tokens, one exactly 1536.
All inputs are finite; a program needn't handle non-finite values.
Results may differ from the reference program's by a relative error of at most 0.00225.
The reference program's roundings to bfloat16 on the way (of `hidden`) count: a program that leaves them out, or rounds other values in their place, can miss the bound.
Values may be sent and summed in bfloat16 or wider, within the bound.
A program may use at most 192 MiB of HBM per device.

```python
import math
import jax
import jax.numpy as jnp
import numpy as np
from jax import lax

D = 3584
FF = 9472
TOKENS = 6144
DOCS = 8
DOC_MOST = 1536


def draw_resid(key, part):
    key_cols = jax.random.fold_in(key, 11)
    key_vals = jax.random.fold_in(key, 23)
    columns = jnp.exp(jax.random.uniform(key_cols, (D,), jnp.float32, 0.0, math.log(10.0))) / 4.6
    base = jnp.clip(jax.random.normal(key_vals, (TOKENS, D), jnp.float32), -6.0, 6.0)
    return (base * columns[None, :]).astype(jnp.bfloat16)


def block_levels(key, dims, cuts, low, largest):
    factor_of, own = 1.0, jax.random.fold_in(key, 6)
    for axis_at, shards_of in cuts:
        draws = jnp.exp(jax.random.uniform(jax.random.fold_in(own, axis_at), (shards_of,), jnp.float32, low / len(cuts), largest / len(cuts)))
        factor_of = factor_of * jnp.repeat(draws, dims[axis_at] // shards_of).reshape([-1 if axis == axis_at else 1 for axis in range(len(dims))])
    return factor_of


def split_up(count, total, reach, lean):
    weights = [(1 << 20) // math.isqrt(rank ** lean) + 1 for rank in range(2, count + 1)]
    surplus, counts = total - reach - (count - 1), [1] * (count - 1)
    while surplus > 0:
        free = [i for i in range(count - 1) if counts[i] < reach]
        pool, remaining = sum([weights[i] for i in free]), surplus
        for i in free:
            more = min(reach - counts[i], max(1, remaining * weights[i] // pool), surplus)
            counts[i] = counts[i] + more
            surplus = surplus - more
    return np.array([reach] + counts)


def uneven(own_key, count, total, most, slope):
    if count == 2:
        one = jax.random.randint(own_key, (), max(1, total - most), min(most, total - 1) + 1)
        return jnp.stack([one, total - one])
    lengths = jnp.asarray(split_up(count, total, most, slope), jnp.int32)
    twos = (count - 1) // 2
    donor, receiver = lengths[1:1 + 2 * twos:2], lengths[2:2 + 2 * twos:2]
    slack = jnp.minimum(donor - 1, most - receiver)
    shifted = jax.random.randint(jax.random.fold_in(own_key, 1), (twos,), 0, 1 << 20) % (slack + 1)
    lengths = lengths.at[1:1 + 2 * twos:2].set(donor - shifted).at[2:2 + 2 * twos:2].set(receiver + shifted)
    return lengths[jax.random.permutation(jax.random.fold_in(own_key, 2), count)]


def noise(stream_key, extent, scale, reach, split=(), dtype=jnp.bfloat16):
    factor_of = block_levels(stream_key, extent, split, -0.22, 0.18) if split else 1.0
    entries = jax.random.normal(stream_key, extent, jnp.float32) * scale * factor_of
    return jnp.minimum(jnp.maximum(entries, -reach), reach).astype(dtype)


def setup_inputs(seed: int = 0, part: int = 0) -> dict:
    keys = jax.random.split(jax.random.key(seed), 9)
    part_keys = jax.random.split(jax.random.fold_in(keys[8], part), 9)
    return {
        "resid": draw_resid(jax.random.fold_in(jax.random.fold_in(keys[8], part), 71), part),
        "gate_pre": noise(part_keys[1], (TOKENS, FF), 1.0, 6.0, ((0, 32),)),
        "up_pre": noise(part_keys[2], (TOKENS, FF), 1.0, 6.0, ((0, 32),)),
        "down_weight": noise(keys[3], (FF, D), FF ** -0.5, 0.0625, ((0, 32),)),
        "norm_gain": jnp.clip(1.0 + 0.18 * jax.random.normal(keys[4], (D,), jnp.float32), 0.1, 1.9),
        "value_head": noise(keys[5], (D,), D ** -0.5, 0.09375, (), jnp.float32),
        "rewards": noise(part_keys[6], (TOKENS,), 0.02, 0.12, ((0, 32),), jnp.float32),
        "seg_ids": jnp.searchsorted(jnp.cumsum(uneven(part_keys[7], DOCS, TOKENS, DOC_MOST, 1)), jnp.arange(TOKENS), side="right").astype(jnp.int32),
    }


EPS = 1e-06

def reference(resid, gate_pre, up_pre, down_weight, norm_gain, value_head, rewards, seg_ids):
    gate = gate_pre.astype(jnp.float32)
    upval = up_pre.astype(jnp.float32)
    sigma = jax.nn.sigmoid(gate)
    active = gate * sigma
    hidden = (active * upval).astype(jnp.bfloat16)
    stream = resid.astype(jnp.float32) + jnp.dot(hidden, down_weight, preferred_element_type=jnp.float32)
    rinv = lax.rsqrt(lax.optimization_barrier(jnp.mean(stream * stream, axis=1)) + EPS)
    head = norm_gain * value_head
    values = lax.optimization_barrier(jnp.sum(stream * head[None, :], axis=1)) * rinv
    totals = jax.ops.segment_sum(rewards, seg_ids, num_segments=DOCS)
    after = jnp.cumsum(totals[::-1])[::-1] - totals
    revsum = jnp.cumsum(rewards[::-1])[::-1]
    returns = revsum - after[seg_ids]
    advantages = returns - values
    grad_value = 64.0 * (values - returns)
    width = stream.shape[1]
    grad_stream = (grad_value * rinv)[:, None] * (head[None, :] - stream * (rinv * values / width)[:, None])
    grad_resid = grad_stream.astype(jnp.bfloat16)
    grad_hidden = lax.dot_general(grad_resid, down_weight, (((1,), (1,)), ((), ())), preferred_element_type=jnp.float32)
    grad_gate = (grad_hidden * upval * sigma * (1.0 + gate * (1.0 - sigma))).astype(jnp.bfloat16)
    grad_up = (grad_hidden * active).astype(jnp.bfloat16)
    return (values, advantages, grad_gate, grad_up, grad_resid)
```

```python
import functools
import jax
import jax.numpy as jnp
from jax import lax
from jax.experimental import pallas as pl
from jax.experimental.pallas import tpu as pltpu
from jax.sharding import PartitionSpec as P

EPS = 1e-06
LANES = 128
CHUNKS = (("plane", "y", 3), ("plane", "x", 3), ("ring", "y", 6), ("ring", "x", 6), ("ring", "y", 5), ("ring", "x", 5))


def chunk_columns(width):
    tiles = width // LANES
    shares = sum(share for _, _, share in CHUNKS)
    edges, done = [0], 0
    for _, _, share in CHUNKS:
        done += share
        edges.append((tiles * done // shares) * LANES)
    edges[-1] = width
    return [(edges[k], edges[k + 1] - edges[k]) for k in range(len(CHUNKS))]


def gather_multiply(columns, hidden_ref, w_ref, full_ref, acc_ref, slots,
                    send_x, send_y, send_up, send_down, send_core, recv, core_recv, slot_sem, own_sem):
    me = lax.axis_index("seq")
    core = lax.rem(me, 2)
    x = lax.rem(lax.div(me, 2), 2)
    y = lax.rem(lax.div(me, 4), 2)
    z = lax.div(me, 8)
    other_core = me + 1 - 2 * core
    at_x = me + 2 - 4 * x
    at_y = me + 4 - 8 * y
    above = me + 8
    below = me - 8
    is_end = 1 - lax.div(z * (3 - z), 2)
    toward = 1 - 2 * lax.div(z, 2)

    def plane_of(turn):
        odd = lax.rem(turn, 2)
        zigzag = odd * lax.div(turn + 1, 2) - (1 - odd) * lax.div(turn, 2)
        return z + toward * (is_end * turn + (1 - is_end) * zigzag)

    def chip_of(dx, dy, turn):
        sx = x + dx - 2 * dx * x
        sy = y + dy - 2 * dy * y
        return plane_of(turn) * 4 + sy * 2 + sx

    def remote(k, src, chip, sends, recvs, target):
        start, size = columns[k]
        shard = 2 * chip + core
        where = full_ref.at[shard, :, pl.ds(start, size)]
        source = where if src is None else src.at[:, pl.ds(start, size)]
        return pltpu.make_async_remote_copy(
            src_ref=source, dst_ref=where, send_sem=sends.at[chip, k], recv_sem=recvs.at[chip, k],
            device_id={"seq": target}, device_id_type=pl.DeviceIdType.MESH)

    def onward(k, dx, dy, turn, act, src=None):
        kind, via, _ = CHUNKS[k]
        chip = chip_of(dx, dy, turn)
        come_from = plane_of(turn)

        def z_copies():
            @pl.when(jnp.logical_and(come_from >= z, z > 0))
            def _():
                act(remote(k, src, chip, send_down, recv, below))

            @pl.when(jnp.logical_and(come_from <= z, z < 3))
            def _():
                act(remote(k, src, chip, send_up, recv, above))

        def plane_copies():
            if dx == 0 and (dy == 0 or via == "x"):
                act(remote(k, src, chip, send_x, recv, at_x))
            if dy == 0 and (dx == 0 or via == "y"):
                act(remote(k, src, chip, send_y, recv, at_y))

        if kind == "ring":
            if dx == 0 and dy == 0:
                z_copies()
            plane_copies()
        else:
            z_copies()

            @pl.when(turn == 0)
            def _():
                plane_copies()
        act(remote(k, src, chip, send_core, core_recv, other_core))

    def arrived(k, dx, dy, turn, recvs):
        chip = chip_of(dx, dy, turn)
        remote(k, None, chip, send_x, recvs, at_x).wait_recv()

    start_it = lambda copy: copy.start()
    wait_it = lambda copy: copy.wait_send()

    barrier = pltpu.get_barrier_semaphore()
    for target in (other_core, at_x, at_y):
        pl.semaphore_signal(barrier, inc=1, device_id={"seq": target}, device_id_type=pl.DeviceIdType.MESH)

    @pl.when(z > 0)
    def _():
        pl.semaphore_signal(barrier, inc=1, device_id={"seq": below}, device_id_type=pl.DeviceIdType.MESH)

    @pl.when(z < 3)
    def _():
        pl.semaphore_signal(barrier, inc=1, device_id={"seq": above}, device_id_type=pl.DeviceIdType.MESH)

    pl.semaphore_wait(barrier, 5 - is_end)

    zero = me * 0
    for k in range(len(columns)):
        onward(k, 0, 0, zero, start_it, w_ref)
    own = pltpu.make_async_copy(w_ref, full_ref.at[me], own_sem)
    own.start()
    acc_ref[...] = jnp.zeros_like(acc_ref)
    own.wait()

    def for_pieces(turn_now, fn):
        def one(t, carry):
            dx = lax.rem(t, 2)
            dy = lax.div(t, 2)
            turn = turn_now - 1 - dx - dy

            @pl.when(jnp.logical_and(turn >= 0, turn <= 3))
            def _():
                fn(t, dx, dy, turn)
            return carry
        lax.fori_loop(0, 4, one, 0)

    def slot_copy(k, t, chip, side):
        start, size = columns[k]
        shard = 2 * chip + (core if side == 0 else 1 - core)
        return pltpu.make_async_copy(
            full_ref.at[shard, :, pl.ds(start, size)], slots.at[2 * t + side, :, pl.ds(0, size)],
            slot_sem.at[2 * t + side])

    def step(turn_now, carry):
        for k in range(len(columns)):
            start, size = columns[k]

            def bring(t, dx, dy, turn):
                arrived(k, dx, dy, turn, core_recv)
                chip = chip_of(dx, dy, turn)
                slot_copy(k, t, chip, 0).start()
                slot_copy(k, t, chip, 1).start()
            for_pieces(turn_now, bring)

            @pl.when(turn_now <= 3)
            def _():
                arrived(k, 0, 0, turn_now, recv)
                onward(k, 0, 0, turn_now, start_it)

            @pl.when(turn_now <= 4)
            def _():
                for dx, dy in ((1, 0), (0, 1)):
                    arrived(k, dx, dy, turn_now - 1, recv)
                    onward(k, dx, dy, turn_now - 1, start_it)

            @pl.when(jnp.logical_and(turn_now >= 2, turn_now <= 5))
            def _():
                arrived(k, 1, 1, turn_now - 2, recv)
                onward(k, 1, 1, turn_now - 2, start_it)

            def multiply(t, dx, dy, turn):
                chip = chip_of(dx, dy, turn)
                slot_copy(k, t, chip, 0).wait()
                slot_copy(k, t, chip, 1).wait()
                near = jnp.dot(hidden_ref[2 * chip + core], slots[2 * t, :, :size],
                               preferred_element_type=jnp.float32)
                far = jnp.dot(hidden_ref[2 * chip + 1 - core], slots[2 * t + 1, :, :size],
                              preferred_element_type=jnp.float32)
                acc_ref[:, start:start + size] += near + far
            for_pieces(turn_now, multiply)
        return carry

    lax.fori_loop(1, 7, step, 0)

    for k in range(len(columns)):
        onward(k, 0, 0, zero, wait_it, w_ref)

    def drain(turn, carry):
        for k in range(len(columns)):
            @pl.when(turn >= 1)
            def _():
                onward(k, 0, 0, turn, wait_it)
            for dx, dy in ((1, 0), (0, 1), (1, 1)):
                onward(k, dx, dy, turn, wait_it)
        return carry

    lax.fori_loop(0, 4, drain, 0)


def gather_and_project(hidden_blocks, weight):
    devices, rows, depth = hidden_blocks.shape
    width = weight.shape[1]
    columns = chunk_columns(width)
    chips = devices // 2
    sems = pltpu.SemaphoreType.DMA((chips, len(columns)))
    return pl.pallas_call(
        functools.partial(gather_multiply, columns),
        out_shape=(
            jax.ShapeDtypeStruct((devices, depth, width), weight.dtype),
            jax.ShapeDtypeStruct((rows, width), jnp.float32),
        ),
        in_specs=[pl.BlockSpec(memory_space=pltpu.VMEM), pl.BlockSpec(memory_space=pl.ANY)],
        out_specs=(pl.BlockSpec(memory_space=pl.ANY), pl.BlockSpec(memory_space=pltpu.VMEM)),
        scratch_shapes=[
            pltpu.VMEM((8, depth, max(size for _, size in columns)), weight.dtype),
            sems, sems, sems, sems, sems, sems, sems,
            pltpu.SemaphoreType.DMA((8,)),
            pltpu.SemaphoreType.DMA(()),
        ],
        compiler_params=pltpu.CompilerParams(
            collective_id=0, has_side_effects=True, vmem_limit_bytes=40 * 1024 * 1024),
        cost_estimate=pl.CostEstimate(
            flops=2 * rows * devices * depth * width,
            bytes_accessed=3 * devices * depth * width * 2, transcendentals=0),
    )(hidden_blocks, weight)


def doc_returns(rewards, seg_ids):
    count = rewards.shape[0]
    first_id = seg_ids[0]
    last_id = seg_ids[count - 1]
    first_total = jnp.sum(jnp.where(seg_ids == first_id, rewards, 0.0))
    own = jnp.stack([first_id.astype(jnp.float32), first_total])
    every = lax.all_gather(own, "seq", axis=0)
    places = lax.broadcasted_iota(jnp.int32, (count, count), 0)
    others = lax.broadcasted_iota(jnp.int32, (count, count), 1)
    same_doc = seg_ids[:, None] == seg_ids[None, :]
    suffix = jnp.logical_and(same_doc, others >= places)
    local_sum = jnp.sum(jnp.where(suffix, rewards[None, :], 0.0), axis=1)
    later = jnp.arange(every.shape[0]) > lax.axis_index("seq")
    joined = jnp.logical_and(later, every[:, 0] == last_id.astype(jnp.float32))
    carried = jnp.sum(jnp.where(joined, every[:, 1], 0.0))
    return local_sum + jnp.where(seg_ids == last_id, carried, 0.0)


def body(in_kernel, resid, gate_pre, up_pre, down_weight, norm_gain, value_head, rewards, seg_ids):
    gate = gate_pre.astype(jnp.float32)
    upval = up_pre.astype(jnp.float32)
    sigma = jax.nn.sigmoid(gate)
    active = gate * sigma
    hidden = (active * upval).astype(jnp.bfloat16)
    returns = doc_returns(rewards, seg_ids)
    if in_kernel:
        rows, depth = hidden.shape[0], down_weight.shape[0]
        blocks = hidden.reshape(rows, hidden.shape[1] // depth, depth).transpose(1, 0, 2)
        down_full, product = gather_and_project(blocks, down_weight)
        down_full = down_full.reshape(hidden.shape[1], down_weight.shape[1])
    else:
        down_full = lax.all_gather(down_weight, "seq", axis=0, tiled=True)
        partial_value = jnp.dot(hidden, down_full, preferred_element_type=jnp.float32)
        product = lax.psum(partial_value, "tp")
    head = norm_gain * value_head
    stream = resid.astype(jnp.float32) + product
    width = stream.shape[1]
    rinv = lax.rsqrt(jnp.mean(stream * stream, axis=1) + EPS)
    values = jnp.sum(stream * head[None, :], axis=1) * rinv
    grad_value = 64.0 * (values - returns)
    grad_stream = (grad_value * rinv)[:, None] * (
        head[None, :] - stream * (rinv * values / width)[:, None]
    )
    grad_resid = grad_stream.astype(jnp.bfloat16)
    grad_hidden = lax.dot_general(
        grad_resid, down_full, (((1,), (1,)), ((), ())), preferred_element_type=jnp.float32
    )
    grad_gate = (grad_hidden * upval * sigma * (1.0 + gate * (1.0 - sigma))).astype(jnp.bfloat16)
    grad_up = (grad_hidden * active).astype(jnp.bfloat16)
    advantages = returns - values
    return (values, advantages, grad_gate, grad_up, grad_resid)


def solution(mesh):
    in_kernel = mesh.shape["groups"] == 1 and mesh.shape["tp"] == 1 and mesh.shape["seq"] == 32
    return jax.shard_map(
        functools.partial(body, in_kernel),
        mesh=mesh,
        in_specs=(
            P(("groups", "seq"), None),
            P(("groups", "seq"), "tp"),
            P(("groups", "seq"), "tp"),
            P(("tp", "seq"), None),
            P(),
            P(),
            P(("groups", "seq")),
            P(("groups", "seq")),
        ),
        out_specs=(
            P(("groups", "seq")),
            P(("groups", "seq")),
            P(("groups", "seq"), "tp"),
            P(("groups", "seq"), "tp"),
            P(("groups", "seq"), None),
        ),
        check_vma=False,
    )
```
